32 devices in a mesh: groups: 2 (over x), bricks: 16 (over z, y, core).
Axes of the slice: x: 2, y: 2, z: 4, core: 2. Of those that a mesh axis runs over, the one named last changes fastest.
Arguments:
- features: bfloat16 [16384, 128], P(('groups', 'bricks')), parts along dimension 0, may hold values from -6 to 6
- conv_weight: bfloat16 [27, 128, 128], replicated, may hold values from -0.109375 to 0.109375
- in_projection: bfloat16 [128, 384], replicated, may hold values from -0.5 to 0.5
- out_projection: bfloat16 [128, 128], replicated, may hold values from -0.5 to 0.5
- head_scale: float32 [2], replicated, may hold values from 3 to 20
- neighbours: int32 [27, 16384], P(None, ('groups', 'bricks')), parts along dimension 1, may hold values from 0 to 640, as said below
- send_rows: int32 [64, 64], P(('groups', 'bricks')), parts along dimension 0, may hold values from 0 to 511, as said below
- send_count: int32 [64], P(('groups', 'bricks')), parts along dimension 0, may hold values from 32 to 64
- window_slot: int32 [16384], P(('groups', 'bricks')), parts along dimension 0, may hold values from 0 to 8191, as said below
- cotangent: bfloat16 [16384, 128], P(('groups', 'bricks')), parts along dimension 0, may hold values from -6 to 6
Outputs:
- mixed: bfloat16 [16384, 128], P(('groups', 'bricks')), parts along dimension 0
- grad_features: bfloat16 [16384, 128], P(('groups', 'bricks')), parts along dimension 0
- grad_conv: float32 [54, 128, 128], P('groups'), parts along dimension 0
- grad_in_projection: float32 [256, 384], P('groups'), parts along dimension 0
- grad_out_projection: float32 [256, 128], P('groups'), parts along dimension 0
The draws below stay inside these ranges and needn't reach their ends.
There are 2 independent parts, one for each index of `groups`. The reference program is written for one: setup_inputs(seed, part) draws one part's arguments, and reference() takes and returns one part's arrays. A program takes and returns all parts, laid end to end along the dimension named above; an argument that names none is the same for every part. Nothing has to cross between parts.
Inputs may be any that keep to these rules, and one draw needn't show every extreme that they name: `neighbours`: in column b * 512 + v: a value below 512 is a voxel of brick b; 512 + j with j below brick b-1's count send_count[2b-1] and 576 + j with j below send_count[2b+2] name received slots; 640 means no neighbour, and is used for every slot of a missing neighbouring brick; offset 27 // 2 names the voxel itself. `send_rows`: each row holds distinct local rows. `window_slot`: A permutation; each brick sends at most 48 of its voxels into the 512 consecutive positions of any one brick, and exactly 48 into some.
All inputs are finite; a program needn't handle non-finite values.
Results may differ from the reference program's by a relative error of at most 0.015.
Values may be sent and summed in bfloat16 or wider, within the bound.
A program may use at most 64 MiB of HBM per device.

```python
import math
import jax
import jax.numpy as jnp
from jax import lax

WIDTH = 128
HEADS = 2
OFFSETS = 27
WIN = 512
V_DEV = 512
HALO = 64
CAP = 48
VOX = 8192
N_BRICKS = 16


def shared_counts(key):
    key = jax.random.fold_in(key, 5)
    first, second = jax.random.split(key)
    counts = jax.random.randint(first, (2 * N_BRICKS,), HALO // 2, HALO + 1)
    full_at = jax.random.randint(second, (), 0, 2 * N_BRICKS)
    return jnp.where(jnp.arange(2 * N_BRICKS) == full_at, HALO, counts).astype(jnp.int32)


def draw_send_count(key, part):
    counts = shared_counts(key)
    return counts


def draw_send_rows(key, part):
    key = jax.random.fold_in(key, 11)
    streams = jax.random.split(key, 2 * N_BRICKS)
    chosen = jax.vmap(lambda stream: jax.random.permutation(stream, V_DEV)[:HALO])(streams)
    return chosen.astype(jnp.int32)


def draw_neighbours(key, part):
    counts = shared_counts(key)
    key = jax.random.fold_in(key, 13)
    streams = jax.random.split(key, 3)
    column = jnp.arange(VOX, dtype=jnp.int32)
    brick = column // V_DEV
    kinds = jax.random.randint(streams[0], (OFFSETS, VOX), 0, 20)
    inside = jax.random.randint(streams[1], (OFFSETS, VOX), 0, V_DEV)
    chooser = jax.random.randint(streams[2], (OFFSETS, VOX), 0, 1 << 20)
    lower_count = counts[jnp.maximum(2 * brick - 1, 0)]
    upper_count = counts[jnp.minimum(2 * brick + 2, 2 * N_BRICKS - 1)]
    absent = V_DEV + 2 * HALO
    lower_slot = jnp.where(brick[None, :] > 0, V_DEV + chooser % lower_count[None, :], absent)
    upper_slot = jnp.where(brick[None, :] < N_BRICKS - 1, V_DEV + HALO + chooser % upper_count[None, :], absent)
    entries = jnp.where(kinds < 6, absent, jnp.where(kinds < 16, inside, jnp.where(kinds < 18, lower_slot, upper_slot)))
    entries = entries.at[OFFSETS // 2].set(column % V_DEV)
    return entries.astype(jnp.int32)


def draw_window_slot(key, part):
    key = jax.random.fold_in(key, 17)
    streams = jax.random.split(key, 4)
    average = V_DEV // N_BRICKS
    excess = CAP - average
    levels = jax.random.randint(streams[0], (N_BRICKS,), 0, excess + 1)
    levels = levels.at[0].set(excess).at[1].set(0)
    deltas = levels - jnp.roll(levels, -1)
    ordering = jax.random.permutation(streams[1], N_BRICKS)
    source = jnp.arange(N_BRICKS)
    counts = average + deltas[(ordering[None, :] - source[:, None]) % N_BRICKS]
    before = jnp.cumsum(counts, axis=0) - counts
    starts = jnp.cumsum(counts, axis=1) - counts
    shuffles = jax.vmap(lambda stream: jax.random.permutation(stream, V_DEV))(jax.random.split(streams[2], N_BRICKS))
    row_orders = jax.vmap(lambda stream: jax.random.permutation(stream, V_DEV))(jax.random.split(streams[3], N_BRICKS))

    def one_source(index, count_row, start_row, before_row, row_order):
        targets = jnp.repeat(jnp.arange(N_BRICKS), count_row, total_repeat_length=V_DEV)
        ranking = jnp.arange(V_DEV) - start_row[targets]
        within = before_row[targets] + ranking
        final = targets * V_DEV + shuffles[targets, within]
        return final[row_order]
    slots = jax.vmap(one_source)(source, counts, starts, before, row_orders)
    return slots.reshape(-1).astype(jnp.int32)


def block_levels(rng, extent, shards, low, top_value):
    def one(position, shards_of):
        steps = jax.random.uniform(jax.random.fold_in(jax.random.fold_in(rng, 6), position), (shards_of,), jnp.float32, low / len(shards), top_value / len(shards))
        return jnp.repeat(jnp.exp(steps), extent[position] // shards_of).reshape((-1,) + (1,) * (len(extent) - position - 1))

    loudness = one(*shards[0])
    for cut in shards[1:]:
        loudness = loudness * one(*cut)
    return loudness


def noise(rng, dims, scale, reach, pieces=(), kind=jnp.bfloat16):
    level = block_levels(rng, dims, pieces, -0.22, 0.18) if pieces else 1.0
    values = jax.random.normal(rng, dims, jnp.float32) * scale * level
    return jnp.minimum(jnp.maximum(values, -reach), reach).astype(kind)


def setup_inputs(seed: int = 0, part: int = 0) -> dict:
    key_list = jax.random.split(jax.random.key(seed), 11)
    own_keys = jax.random.split(jax.random.fold_in(key_list[10], part), 11)
    return {
        "features": noise(own_keys[0], (VOX, WIDTH), 1.0, 6.0, ((0, 16),)),
        "conv_weight": noise(key_list[1], (OFFSETS, WIDTH, WIDTH), (OFFSETS * WIDTH) ** -0.5, 0.109375),
        "in_projection": noise(key_list[2], (WIDTH, 3 * WIDTH), WIDTH ** -0.5, 0.5),
        "out_projection": noise(key_list[3], (WIDTH, WIDTH), WIDTH ** -0.5, 0.5),
        "head_scale": jnp.clip(jnp.exp(jax.random.uniform(key_list[4], (HEADS,), jnp.float32, math.log(3.0), math.log(20.0))), 3.0, 20.0),
        "neighbours": draw_neighbours(jax.random.fold_in(jax.random.fold_in(key_list[10], part), 71), part),
        "send_rows": draw_send_rows(jax.random.fold_in(jax.random.fold_in(key_list[10], part), 71), part),
        "send_count": draw_send_count(jax.random.fold_in(jax.random.fold_in(key_list[10], part), 71), part),
        "window_slot": draw_window_slot(jax.random.fold_in(jax.random.fold_in(key_list[10], part), 71), part),
        "cotangent": noise(own_keys[9], (VOX, WIDTH), 1.0, 6.0, ((0, 16),)),
    }


EPS = 1e-06

def settle(values):
    return lax.optimization_barrier(values.astype(jnp.bfloat16)).astype(jnp.float32)

def attention_core(projected, head_scale):
    windows = projected.shape[0] // WIN
    heads_view = projected.astype(jnp.float32).reshape(windows, WIN, 3, HEADS, WIDTH // HEADS)
    query_part = heads_view[:, :, 0]
    key_part = heads_view[:, :, 1]
    value_part = heads_view[:, :, 2]
    query_part = query_part * lax.rsqrt(lax.optimization_barrier(jnp.sum(query_part * query_part, axis=-1, keepdims=True)) + EPS) * head_scale[:, None]
    key_part = key_part * lax.rsqrt(lax.optimization_barrier(jnp.sum(key_part * key_part, axis=-1, keepdims=True)) + EPS)
    scores = jnp.einsum('wqhd,wkhd->whqk', settle(query_part), settle(key_part))
    weights = jnp.exp(scores)
    weights = settle(weights / lax.optimization_barrier(jnp.sum(weights, axis=-1, keepdims=True)))
    mixed_rows = jnp.einsum('whqk,wkhd->wqhd', weights, value_part)
    return mixed_rows.reshape(windows * WIN, WIDTH).astype(jnp.bfloat16)

def reference(features, conv_weight, in_projection, out_projection, head_scale, neighbours, send_rows, send_count, window_slot, cotangent):
    blocks = features.reshape(N_BRICKS, V_DEV, WIDTH)
    lists = send_rows.reshape(N_BRICKS, 2, HALO)
    present = jnp.arange(HALO)[None, None, :] < send_count.reshape(N_BRICKS, 2)[:, :, None]
    border = jax.vmap(lambda source, chosen: jnp.take(source, chosen, axis=0))(blocks, lists)
    border = jnp.where(present[:, :, :, None], border, jnp.zeros((), jnp.bfloat16))
    empty = jnp.zeros((1, HALO, WIDTH), jnp.bfloat16)
    from_lower = jnp.concatenate([empty, border[:-1, 1]], axis=0)
    from_upper = jnp.concatenate([border[1:, 0], empty], axis=0)
    tables = jnp.concatenate([blocks, from_lower, from_upper, jnp.zeros((N_BRICKS, 1, WIDTH), jnp.bfloat16)], axis=1)
    picked = neighbours.reshape(OFFSETS, N_BRICKS, V_DEV).transpose(1, 0, 2)
    kernel = conv_weight.astype(jnp.float32)

    def convolve(couple):
        brick_table, chosen = couple
        gathered = jnp.take(brick_table, chosen, axis=0).astype(jnp.float32)
        return jnp.einsum('kvc,kco->vo', gathered, kernel)
    filtered = lax.map(convolve, (tables, picked))
    activated = jax.nn.silu(filtered).astype(jnp.bfloat16).reshape(VOX, WIDTH)
    activated_win = jnp.zeros((VOX, WIDTH), jnp.bfloat16).at[window_slot].set(activated)
    grad_win = jnp.zeros((VOX, WIDTH), jnp.bfloat16).at[window_slot].set(cotangent)

    def attend(couple):
        window_rows, grad_rows = couple
        projected = lax.optimization_barrier(jnp.dot(window_rows, in_projection, preferred_element_type=jnp.float32).astype(jnp.bfloat16))
        core, pullback = jax.vjp(lambda packed_in: attention_core(packed_in, head_scale), projected)
        mixed_rows = jnp.dot(core, out_projection, preferred_element_type=jnp.float32).astype(jnp.bfloat16)
        grad_core = jnp.dot(grad_rows, out_projection.T, preferred_element_type=jnp.float32).astype(jnp.bfloat16)
        grad_projected = pullback(grad_core)[0]
        grad_back = jnp.dot(grad_projected, in_projection.T, preferred_element_type=jnp.float32).astype(jnp.bfloat16)
        in_part = jnp.dot(window_rows.T, grad_projected, preferred_element_type=jnp.float32)
        out_part = jnp.dot(core.T, grad_rows, preferred_element_type=jnp.float32)
        return (mixed_rows, grad_back, in_part, out_part)
    mixed_win, grad_back_win, in_parts, out_parts = lax.map(attend, (activated_win.reshape(N_BRICKS, V_DEV, WIDTH), grad_win.reshape(N_BRICKS, V_DEV, WIDTH)))
    mixed = mixed_win.reshape(VOX, WIDTH)[window_slot]
    grad_activated = grad_back_win.reshape(VOX, WIDTH)[window_slot].reshape(N_BRICKS, V_DEV, WIDTH)
    sigmoid = jax.nn.sigmoid(filtered)
    grad_filtered = (grad_activated.astype(jnp.float32) * (sigmoid * (1.0 + filtered * (1.0 - sigmoid)))).astype(jnp.bfloat16)

    def transpose_conv(triple):
        brick_table, chosen, grad_rows = triple
        gathered = jnp.take(brick_table, chosen, axis=0).astype(jnp.float32)
        grad_rows = grad_rows.astype(jnp.float32)
        kernel_grad = jnp.einsum('kvc,vo->kco', gathered, grad_rows)
        contrib = jnp.einsum('vo,kco->kvc', grad_rows, kernel)
        spread = jnp.zeros((V_DEV + 2 * HALO + 1, WIDTH), jnp.float32).at[chosen.reshape(-1)].add(contrib.reshape(-1, WIDTH))
        return (spread, kernel_grad)
    spreads, kernel_grads = lax.map(transpose_conv, (tables, picked, grad_filtered))
    local_part = spreads[:, :V_DEV]
    lower_slots = spreads[:, V_DEV:V_DEV + HALO]
    upper_slots = spreads[:, V_DEV + HALO:V_DEV + 2 * HALO]
    zero_slots = jnp.zeros((1, HALO, WIDTH), jnp.float32)
    back_lower = jnp.concatenate([zero_slots, upper_slots[:-1]], axis=0)
    back_upper = jnp.concatenate([lower_slots[1:], zero_slots], axis=0)
    back_lower = jnp.where(present[:, 0, :, None], back_lower, 0.0)
    back_upper = jnp.where(present[:, 1, :, None], back_upper, 0.0)

    def settle_rows(local_rows, chosen, lower_rows, upper_rows):
        return local_rows.at[chosen[0]].add(lower_rows).at[chosen[1]].add(upper_rows)
    grad_features = jax.vmap(settle_rows)(local_part, lists, back_lower, back_upper).reshape(VOX, WIDTH).astype(jnp.bfloat16)
    factor = VOX ** (-0.5)
    return (mixed, grad_features, lax.optimization_barrier(jnp.sum(kernel_grads, axis=0)) * factor, lax.optimization_barrier(jnp.sum(in_parts, axis=0)) * factor, lax.optimization_barrier(jnp.sum(out_parts, axis=0)) * factor)
```

```python
import functools

import jax
import jax.numpy as jnp
from jax import lax
from jax.experimental import pallas as pl
from jax.experimental.pallas import tpu as pltpu
from jax.sharding import PartitionSpec as P

HEADS = 2
EPS = 1e-06
F32 = jnp.float32
BF16 = jnp.bfloat16
VMEM = pl.BlockSpec(memory_space=pltpu.VMEM)
SMEM = pl.BlockSpec(memory_space=pltpu.SMEM)


def dot(a, b, ca=1, cb=0):
    return lax.dot_general(a, b, (((ca,), (cb,)), ((), ())), preferred_element_type=F32)


def iota(shape, dim):
    return lax.broadcasted_iota(jnp.int32, shape, dim)


def select_rows(rows, lane_index):
    shape = (rows, lane_index.shape[1])
    return jnp.where(iota(shape, 0) == lane_index, 1.0, 0.0).astype(BF16)


def rank_plan(slot, devices, cap):
    height = slot.shape[1]
    bits = height.bit_length() - 1
    target = lax.shift_right_logical(slot, jnp.full_like(slot, bits))
    within = slot & (height - 1)
    member = iota((devices, height), 0) == target
    before = jnp.where(iota((height, height), 0) < iota((height, height), 1), 1.0, 0.0).astype(BF16)
    ones = jnp.where(member, 1.0, 0.0)
    counts = dot(ones.astype(BF16), before)
    rank = jnp.sum(counts * ones, axis=0, keepdims=True).astype(jnp.int32)
    return target, within, rank, target * cap + rank


def position_rows(target, within, rank, me, devices, cap):
    slots = devices * cap
    height = target.shape[1]
    where_to = select_rows(slots, rank + me * cap)
    shown = within + 1
    hit = iota((devices, height), 0) == target
    high = jnp.where(hit, lax.shift_right_logical(shown, jnp.full_like(shown, 8)), 0)
    low = jnp.where(hit, shown & 255, 0)
    return (
        dot(high.astype(F32).astype(BF16), where_to, 1, 1),
        dot(low.astype(F32).astype(BF16), where_to, 1, 1),
    )


def border_select(send, count0, count1, height):
    both = send.shape[1]
    lane = iota((1, both), 1)
    limit = jnp.where(lane < both // 2, count0, count1 + both // 2)
    return select_rows(height, jnp.where(lane < limit, send, -1))


def attention(win, grad_win, in_proj, out_proj, scale):
    width = win.shape[1]
    dim = width // HEADS
    projected = dot(in_proj, win, 0, 1).astype(BF16).astype(F32)
    grad_core = dot(out_proj, grad_win, 1, 1).astype(BF16)
    cores, grads = [], [[], [], []]
    for h in range(HEADS):
        q = projected[h * dim : (h + 1) * dim]
        k = projected[width + h * dim : width + (h + 1) * dim]
        v = projected[2 * width + h * dim : 2 * width + (h + 1) * dim].astype(BF16)
        rq = lax.rsqrt(jnp.sum(q * q, axis=0, keepdims=True) + EPS)
        rk = lax.rsqrt(jnp.sum(k * k, axis=0, keepdims=True) + EPS)
        qp = (q * rq * scale[h]).astype(BF16)
        kp = (k * rk).astype(BF16)
        grad_h = grad_core[h * dim : (h + 1) * dim]
        e = jnp.exp(dot(kp, qp, 0, 0))
        p = e * (1.0 / jnp.sum(e, axis=0, keepdims=True))
        w = p.astype(BF16)
        cores.append(dot(v, w).astype(BF16))
        dw = dot(v, grad_h, 0, 0).astype(BF16).astype(F32)
        dv = dot(grad_h, w, 1, 1)
        ds = (p * (dw - jnp.sum(dw * p, axis=0, keepdims=True))).astype(BF16)
        dqp = dot(kp, ds).astype(BF16).astype(F32)
        dkp = dot(qp, ds, 1, 1).astype(BF16).astype(F32)
        dq = scale[h] * rq * (dqp - q * (rq * rq) * jnp.sum(dqp * q, axis=0, keepdims=True))
        dk = rk * (dkp - k * (rk * rk) * jnp.sum(dkp * k, axis=0, keepdims=True))
        grads[0].append(dq.astype(BF16))
        grads[1].append(dk.astype(BF16))
        grads[2].append(dv.astype(BF16))
    core = jnp.concatenate(cores, axis=0)
    grad_projected = jnp.concatenate(grads[0] + grads[1] + grads[2], axis=0)
    mixed = dot(out_proj, core, 0, 0).astype(BF16)
    grad_back = dot(in_proj, grad_projected).astype(BF16)
    grad_in = dot(win, grad_projected, 0, 1)
    grad_out = dot(core, grad_win)
    return mixed, grad_back, grad_in, grad_out


def start_kernel(devices, cap, halo, feat, cot, slot, send, count, place, message, border, stage):
    me = lax.axis_index("bricks")
    height = feat.shape[0]
    slots = devices * cap
    target, within, rank, placing = rank_plan(slot[...], devices, cap)
    place[...] = placing
    chosen = border_select(send[...], count[0], count[1], height)
    border[...] = dot(chosen, feat[...], 0, 0).astype(BF16)
    rows = dot(select_rows(slots, placing), cot[...])
    message[:, :cap, :] = rows.astype(BF16).reshape(devices, cap, -1)
    high, low = position_rows(target, within, rank, me, devices, cap)
    stage[...] = jnp.zeros_like(stage)
    chunks = slots // 128
    for r in range(chunks):
        stage[:, r, :] = high[:, r * 128 : (r + 1) * 128]
        stage[:, chunks + r, :] = low[:, r * 128 : (r + 1) * 128]
    message[:, cap:, :] = stage[...].astype(BF16)


def conv_kernel(feat, halo, near, weight, slot, filtered, sent, gathered, table):
    height, width = feat.shape
    offsets = near.shape[0]
    slots = sent.shape[0]
    both = jnp.concatenate([feat[...], halo[...]], axis=0)
    table[...] = both.astype(F32).T.astype(BF16)

    def step(k, carry):
        chosen = select_rows(both.shape[0], near[pl.ds(k, 1), :])
        at = pl.ds(pl.multiple_of(k * width, width), width)
        gathered[at, :] = dot(table[...], chosen).astype(BF16)
        return carry

    lax.fori_loop(0, offsets, step, 0)
    total = dot(weight[...], gathered[...], 0, 0)
    filtered[...] = total
    activated = (total * jax.nn.sigmoid(total)).astype(BF16)
    sent[...] = dot(activated, select_rows(slots, slot[...]), 1, 1).T.astype(BF16)


def window_call(cap, act, cot, in_proj, out_proj, scale, mixed_out, grad_back_out, grad_in, grad_out, height):
    devices = cot.shape[0]
    slots = devices * cap
    chunks = slots // 128
    marks = jnp.sum(cot[:, cap:, :].astype(F32), axis=0)
    landing = jnp.concatenate(
        [marks[r : r + 1] * 256.0 + marks[chunks + r : chunks + r + 1] for r in range(chunks)], axis=1
    ).astype(jnp.int32) - 1
    chosen = select_rows(height, landing)
    win = dot(chosen, act[...]).astype(BF16)
    grad_win = dot(chosen, cot[:, :cap, :].reshape(slots, -1)).astype(BF16)
    mixed, grad_back, grad_i, grad_o = attention(
        win, grad_win, in_proj[...], out_proj[...], (scale[0], scale[1])
    )
    mixed_out[...] = dot(mixed, chosen).T.astype(BF16)
    grad_back_out[...] = dot(grad_back, chosen).T.astype(BF16)
    grad_in[...] = grad_i
    grad_out[...] = grad_o


def brick_kernel(
    height, mixed_in, back_in, place, filtered, gathered, near, weight,
    mixed, kernel_grad, spread, grads,
):
    offsets = near.shape[0]
    width = filtered.shape[0]
    chosen = select_rows(mixed_in.shape[0], place[...])
    mixed[...] = dot(mixed_in[...], chosen, 0, 0).T.astype(BF16)
    grad_act = dot(back_in[...], chosen, 0, 0)
    f = filtered[...]
    sigmoid = jax.nn.sigmoid(f)
    grad = (grad_act * (sigmoid * (1.0 + f * (1.0 - sigmoid)))).T.astype(BF16)
    grads[...] = grad
    kernel_grad[...] = dot(gathered[...], grad)
    spread[...] = jnp.zeros_like(spread)

    def step(k, carry):
        at = pl.ds(pl.multiple_of(k * width, width), width)
        contrib = dot(grads[...], weight[at, :], 1, 1).astype(BF16)
        spread[...] += dot(select_rows(spread.shape[0], near[pl.ds(k, 1), :]), contrib)
        return carry

    lax.fori_loop(0, offsets, step, 0)


def finish_kernel(local, back, send, count, out):
    chosen = border_select(send[...], count[0], count[1], local.shape[0])
    out[...] = (local[...] + dot(chosen, back[...])).astype(BF16)


def shape(dims, kind):
    return jax.ShapeDtypeStruct(dims, kind)


def params():
    return pltpu.CompilerParams(vmem_limit_bytes=48 * 1024 * 1024)


def swap(low, high):
    devices = lax.axis_size("bricks")
    up = [(i, i + 1) for i in range(devices - 1)]
    down = [(j, i) for i, j in up]
    return lax.ppermute(high, "bricks", up), lax.ppermute(low, "bricks", down)


def exchange(array):
    return lax.all_to_all(array, "bricks", split_axis=0, concat_axis=0, tiled=True)


def body(
    features, conv_weight, in_projection, out_projection, head_scale,
    neighbours, send_rows, send_count, window_slot, cotangent,
):
    height, width = features.shape
    halo = send_rows.shape[1]
    offsets = neighbours.shape[0]
    devices = lax.axis_size("bricks")
    capacity = height // devices + height // devices // 2
    cap = -(-capacity // 16) * 16
    slots = devices * cap
    slot = window_slot.reshape(1, height)
    send = send_rows.reshape(1, 2 * halo)
    weight = conv_weight.reshape(offsets * width, width)
    place, message, border = pl.pallas_call(
        functools.partial(start_kernel, devices, cap, halo),
        out_shape=(
            shape((1, height), jnp.int32),
            shape((devices, cap + 16, width), BF16),
            shape((2 * halo, width), BF16),
        ),
        in_specs=[VMEM] * 4 + [SMEM],
        out_specs=[VMEM] * 3,
        scratch_shapes=[pltpu.VMEM((devices, 16, 128), F32)],
        compiler_params=params(),
    )(features, cotangent, slot, send, send_count)
    cot = exchange(message)
    lower, upper = swap(border[:halo], border[halo:])
    filtered, sent, gathered = pl.pallas_call(
        conv_kernel,
        out_shape=(
            shape((width, height), F32),
            shape((slots, width), BF16),
            shape((offsets * width, height), BF16),
        ),
        in_specs=[VMEM] * 5,
        out_specs=[VMEM] * 3,
        scratch_shapes=[pltpu.VMEM((width, height + 2 * halo), BF16)],
        compiler_params=params(),
    )(features, jnp.concatenate([lower, upper], axis=0), neighbours, weight, place)
    act = exchange(sent.reshape(devices, cap, width)).reshape(slots, width)

    def window(*refs):
        window_call(cap, *refs, height=height)

    mixed_back, grad_back, grad_in, grad_out = pl.pallas_call(
        window,
        out_shape=(
            shape((slots, width), BF16),
            shape((slots, width), BF16),
            shape(in_projection.shape, F32),
            shape(out_projection.shape, F32),
        ),
        in_specs=[VMEM] * 4 + [SMEM],
        out_specs=[VMEM] * 4,
        compiler_params=params(),
    )(act, cot, in_projection, out_projection, head_scale)
    grad_back = exchange(grad_back.reshape(devices, cap, width)).reshape(slots, width)
    mixed_back = exchange(mixed_back.reshape(devices, cap, width)).reshape(slots, width)
    mixed, kernel_grad, spread = pl.pallas_call(
        functools.partial(brick_kernel, height),
        out_shape=(
            shape((height, width), BF16),
            shape((offsets * width, width), F32),
            shape((height + 2 * halo, width), F32),
        ),
        in_specs=[VMEM] * 7,
        out_specs=[VMEM] * 3,
        scratch_shapes=[pltpu.VMEM((height, width), BF16)],
        compiler_params=params(),
    )(mixed_back, grad_back, place, filtered, gathered, neighbours, weight)
    totals = lax.psum((kernel_grad, grad_in, grad_out), "bricks")
    edge = spread[height:].astype(BF16)
    low_back, high_back = swap(edge[:halo], edge[halo:])
    grad_features = pl.pallas_call(
        finish_kernel,
        out_shape=shape((height, width), BF16),
        in_specs=[VMEM] * 3 + [SMEM],
        out_specs=VMEM,
        compiler_params=params(),
    )(spread[:height], jnp.concatenate([low_back, high_back], axis=0), send, send_count)
    factor = (height * devices) ** (-0.5)
    return (
        mixed,
        grad_features,
        totals[0].reshape(conv_weight.shape) * factor,
        totals[1] * factor,
        totals[2] * factor,
    )


def solution(mesh):
    return jax.shard_map(
        body,
        mesh=mesh,
        in_specs=(
            P(("groups", "bricks"), None),
            P(),
            P(),
            P(),
            P(),
            P(None, ("groups", "bricks")),
            P(("groups", "bricks"), None),
            P(("groups", "bricks")),
            P(("groups", "bricks")),
            P(("groups", "bricks"), None),
        ),
        out_specs=(
            P(("groups", "bricks"), None),
            P(("groups", "bricks"), None),
            P("groups", None, None),
            P("groups", None),
            P("groups", None),
        ),
        check_vma=False,
    )
```

```python
import functools

import jax
import jax.numpy as jnp
from jax import lax
from jax.experimental import pallas as pl
from jax.experimental.pallas import tpu as pltpu
from jax.sharding import PartitionSpec as P

HEADS = 2
EPS = 1e-06
F32 = jnp.float32
BF16 = jnp.bfloat16
VMEM = pl.BlockSpec(memory_space=pltpu.VMEM)
SMEM = pl.BlockSpec(memory_space=pltpu.SMEM)


def dot(a, b, ca=1, cb=0):
    return lax.dot_general(a, b, (((ca,), (cb,)), ((), ())), preferred_element_type=F32)


def iota(shape, dim):
    return lax.broadcasted_iota(jnp.int32, shape, dim)


def select_rows(rows, lane_index):
    shape = (rows, lane_index.shape[1])
    return jnp.where(iota(shape, 0) == lane_index, 1.0, 0.0).astype(BF16)


def rank_plan(slot, devices, cap):
    height = slot.shape[1]
    bits = height.bit_length() - 1
    target = lax.shift_right_logical(slot, jnp.full_like(slot, bits))
    within = slot & (height - 1)
    member = iota((devices, height), 0) == target
    before = jnp.where(iota((height, height), 0) < iota((height, height), 1), 1.0, 0.0).astype(BF16)
    ones = jnp.where(member, 1.0, 0.0)
    counts = dot(ones.astype(BF16), before)
    rank = jnp.sum(counts * ones, axis=0, keepdims=True).astype(jnp.int32)
    return target, within, rank, target * cap + rank


def position_rows(target, within, rank, me, devices, cap):
    slots = devices * cap
    height = target.shape[1]
    where_to = select_rows(slots, rank + me * cap)
    shown = within + 1
    hit = iota((devices, height), 0) == target
    high = jnp.where(hit, lax.shift_right_logical(shown, jnp.full_like(shown, 8)), 0)
    low = jnp.where(hit, shown & 255, 0)
    return (
        dot(high.astype(F32).astype(BF16), where_to, 1, 1),
        dot(low.astype(F32).astype(BF16), where_to, 1, 1),
    )


def border_select(send, count0, count1, height):
    both = send.shape[1]
    lane = iota((1, both), 1)
    limit = jnp.where(lane < both // 2, count0, count1 + both // 2)
    return select_rows(height, jnp.where(lane < limit, send, -1))


def heads_forward(projected, scale):
    width = projected.shape[0] // 3
    dim = width // HEADS
    kept = []
    for h in range(HEADS):
        q = projected[h * dim : (h + 1) * dim]
        k = projected[width + h * dim : width + (h + 1) * dim]
        v = projected[2 * width + h * dim : 2 * width + (h + 1) * dim].astype(BF16)
        rq = lax.rsqrt(jnp.sum(q * q, axis=0, keepdims=True) + EPS)
        rk = lax.rsqrt(jnp.sum(k * k, axis=0, keepdims=True) + EPS)
        qp = (q * rq * scale[h]).astype(BF16)
        kp = (k * rk).astype(BF16)
        e = jnp.exp(dot(kp, qp, 0, 0))
        p = e * (1.0 / jnp.sum(e, axis=0, keepdims=True))
        w = p.astype(BF16)
        kept.append((q, k, v, rq, rk, qp, kp, p, w, dot(v, w).astype(BF16)))
    return kept


def heads_backward(kept, grad_core, scale):
    grads = [[], [], []]
    for h in range(HEADS):
        q, k, v, rq, rk, qp, kp, p, w, _ = kept[h]
        dim = q.shape[0]
        grad_h = grad_core[h * dim : (h + 1) * dim]
        dw = dot(v, grad_h, 0, 0).astype(BF16).astype(F32)
        dv = dot(grad_h, w, 1, 1)
        ds = (p * (dw - jnp.sum(dw * p, axis=0, keepdims=True))).astype(BF16)
        dqp = dot(kp, ds).astype(BF16).astype(F32)
        dkp = dot(qp, ds, 1, 1).astype(BF16).astype(F32)
        dq = scale[h] * rq * (dqp - q * (rq * rq) * jnp.sum(dqp * q, axis=0, keepdims=True))
        dk = rk * (dkp - k * (rk * rk) * jnp.sum(dkp * k, axis=0, keepdims=True))
        grads[0].append(dq.astype(BF16))
        grads[1].append(dk.astype(BF16))
        grads[2].append(dv.astype(BF16))
    return jnp.concatenate(grads[0] + grads[1] + grads[2], axis=0)


class Exchange:
    def __init__(self, devices, me, out, into, sems, which):
        self.devices, self.me, self.out, self.into = devices, me, out, into
        self.send, self.recv = sems.at[2 * which], sems.at[2 * which + 1]

    def start(self):
        def step(s, carry):
            to = lax.rem(self.me + s, self.devices)
            pltpu.make_async_remote_copy(
                src_ref=self.out.at[to],
                dst_ref=self.into.at[self.me],
                send_sem=self.send,
                recv_sem=self.recv,
                device_id={"bricks": to},
                device_id_type=pl.DeviceIdType.MESH,
            ).start()
            return carry

        lax.fori_loop(1, self.devices, step, 0)
        self.into[self.me] = self.out[self.me]

    def wait_recv(self):
        part = self.into.at[pl.ds(0, self.devices - 1)]
        pltpu.make_async_copy(part, part, self.recv).wait()

    def wait_send(self):
        part = self.out.at[pl.ds(0, self.devices - 1)]
        pltpu.make_async_copy(part, part, self.send).wait()


class Edges:
    def __init__(self, devices, me, out, into, sems):
        self.has = (me > 0, me < devices - 1)
        self.into = into
        self.copies = [
            pltpu.make_async_remote_copy(
                src_ref=out.at[side],
                dst_ref=into.at[1 - side],
                send_sem=sems.at[side],
                recv_sem=sems.at[2 + 1 - side],
                device_id={"bricks": lax.rem(me + step + devices, devices)},
                device_id_type=pl.DeviceIdType.MESH,
            )
            for side, step in ((0, -1), (1, 1))
        ]

    def blank(self):
        for side in range(2):
            @pl.when(jnp.logical_not(self.has[side]))
            def _():
                self.into[side] = jnp.zeros(self.into.shape[1:], self.into.dtype)

    def start(self):
        for side in range(2):
            @pl.when(self.has[side])
            def _():
                self.copies[side].start()

    def wait(self):
        for side in range(2):
            @pl.when(self.has[side])
            def _():
                self.copies[side].wait_send()
                self.copies[1 - side].wait_recv()


def level_kernel(
    devices, cap, halo, total_rows, factor,
    feat, weight, in_proj, out_proj, near, send, slot, cot, scale, count,
    mixed, grad_features, gathered_grads,
    stage, chosen, gathered, contrib, filtered, local, partial, summed,
    cot_out, cot_in, act_out, act_in, back_out, back_in, mix_out, mix_in,
    halo_out, halo_in, edge_out, edge_in, half_out, half_in,
    sems, halo_sems, edge_sems, half_sems, full_sems,
):
    me = lax.axis_index("bricks")
    height, width = feat.shape
    offsets = near.shape[0]
    slots = devices * cap
    chunks = slots // 128
    table_rows = height + 2 * halo
    barrier = pltpu.get_barrier_semaphore()
    halos = Edges(devices, me, halo_out, halo_in, halo_sems)
    edges = Edges(devices, me, edge_out, edge_in, edge_sems)
    halos.blank()
    edges.blank()

    def greet(s, carry):
        pl.semaphore_signal(
            barrier,
            inc=1,
            device_id={"bricks": lax.rem(me + s, devices)},
            device_id_type=pl.DeviceIdType.MESH,
        )
        return carry

    lax.fori_loop(1, devices, greet, 0)
    cots = Exchange(devices, me, cot_out, cot_in, sems, 0)
    acts = Exchange(devices, me, act_out, act_in, sems, 1)
    backs = Exchange(devices, me, back_out, back_in, sems, 2)
    mixes = Exchange(devices, me, mix_out, mix_in, sems, 3)

    border = border_select(send[...], count[0], count[1], height)
    halo_out[...] = dot(border, feat[...], 0, 0).astype(BF16).reshape(2, halo, width)
    pl.semaphore_wait(barrier, devices - 1)
    halos.start()

    target, within, rank, placing = rank_plan(slot[...], devices, cap)
    to_slots = select_rows(slots, placing)
    cot_out[:, :cap, :] = dot(to_slots, cot[...]).astype(BF16).reshape(devices, cap, width)
    high, low = position_rows(target, within, rank, me, devices, cap)
    stage[...] = jnp.zeros_like(stage)
    for r in range(chunks):
        stage[:, r, :] = high[:, r * 128 : (r + 1) * 128]
        stage[:, chunks + r, :] = low[:, r * 128 : (r + 1) * 128]
    cot_out[:, cap:, :] = stage[...].astype(BF16)
    cots.start()

    def choose(k, carry):
        at = pl.ds(pl.multiple_of(k * height, height), height)
        chosen[:, at] = select_rows(table_rows, near[pl.ds(k, 1), :])
        return carry

    lax.fori_loop(0, offsets, choose, 0)
    halos.wait()
    table = jnp.concatenate(
        [feat[...].astype(F32).T, halo_in[...].reshape(2 * halo, width).astype(F32).T], axis=1
    ).astype(BF16)

    def gather(k, carry):
        at = pl.ds(pl.multiple_of(k * height, height), height)
        rows = pl.ds(pl.multiple_of(k * width, width), width)
        gathered[rows, :] = dot(table, chosen[:, at]).astype(BF16)
        return carry

    lax.fori_loop(0, offsets, gather, 0)
    total = dot(weight[...], gathered[...], 0, 0)
    filtered[...] = total
    activated = (total * jax.nn.sigmoid(total)).astype(BF16)
    act_out[...] = dot(to_slots, activated, 1, 1).astype(BF16).reshape(devices, cap, width)
    acts.start()

    cots.wait_recv()
    marks = jnp.sum(cot_in[:, cap:, :].astype(F32), axis=0)
    landing = jnp.concatenate(
        [marks[r : r + 1] * 256.0 + marks[chunks + r : chunks + r + 1] for r in range(chunks)], axis=1
    ).astype(jnp.int32) - 1
    to_window = select_rows(height, landing)
    grad_win = dot(to_window, cot_in[:, :cap, :].reshape(slots, width)).astype(BF16)
    grad_core = dot(out_proj[...], grad_win, 1, 1).astype(BF16)
    scales = (scale[0], scale[1])
    acts.wait_recv()
    win = dot(to_window, act_in[...].reshape(slots, width)).astype(BF16)
    projected = dot(in_proj[...], win, 0, 1).astype(BF16).astype(F32)
    kept = heads_forward(projected, scales)
    grad_projected = heads_backward(kept, grad_core, scales)
    grad_back = dot(in_proj[...], grad_projected).astype(BF16)
    back_out[...] = dot(grad_back, to_window).T.astype(BF16).reshape(devices, cap, width)
    backs.start()
    core = jnp.concatenate([kept[h][-1] for h in range(HEADS)], axis=0)
    mixed_win = dot(out_proj[...], core, 0, 0).astype(BF16)
    mix_out[...] = dot(mixed_win, to_window).T.astype(BF16).reshape(devices, cap, width)
    base = offsets * width
    grad_in = dot(win, grad_projected, 0, 1)
    parts = in_proj.shape[1] // width
    for j in range(parts):
        partial[base + j * width : base + (j + 1) * width] = grad_in[:, j * width : (j + 1) * width]
    base += parts * width
    partial[base : base + width] = dot(core, grad_win)
    base += width
    partial[base:] = jnp.zeros((total_rows - base, width), F32)

    f = filtered[...]
    sigmoid = jax.nn.sigmoid(f)
    slope = sigmoid * (1.0 + f * (1.0 - sigmoid))
    backs.wait_recv()
    grad_act = dot(back_in[...].reshape(slots, width), to_slots, 0, 0)
    grad = (grad_act * slope).T.astype(BF16)
    partial[: offsets * width] = dot(gathered[...], grad)

    bits = devices.bit_length() - 1
    at, length, offset = 0, total_rows, 0
    places = []

    def halving(b, at, length, offset):
        length = length // 2
        bit = lax.rem(me // (1 << b), 2)
        other = me + (1 - 2 * bit) * (1 << b)
        keep = pl.multiple_of(at + bit * length, 16)
        give = pl.multiple_of(at + (1 - bit) * length, 16)
        half_out[offset : offset + length] = partial[pl.ds(give, length)].astype(BF16)
        copy = pltpu.make_async_remote_copy(
            src_ref=half_out.at[pl.ds(offset, length)],
            dst_ref=half_in.at[pl.ds(offset, length)],
            send_sem=half_sems.at[2 * b],
            recv_sem=half_sems.at[2 * b + 1],
            device_id={"bricks": other},
            device_id_type=pl.DeviceIdType.MESH,
        )
        copy.start()
        return copy, keep, length

    def doubling(b, at, length):
        bit = lax.rem(me // (1 << b), 2)
        other = me + (1 - 2 * bit) * (1 << b)
        part = summed.at[pl.ds(pl.multiple_of(at, 16), length)]
        copy = pltpu.make_async_remote_copy(
            src_ref=part,
            dst_ref=part,
            send_sem=full_sems.at[2 * b],
            recv_sem=full_sems.at[2 * b + 1],
            device_id={"bricks": other},
            device_id_type=pl.DeviceIdType.MESH,
        )
        copy.start()
        return copy

    def contribution(k, carry):
        rows = pl.ds(pl.multiple_of(k * height, height), height)
        taps = pl.ds(pl.multiple_of(k * width, width), width)
        contrib[rows, :] = dot(grad, weight[taps, :], 1, 1).astype(BF16)
        return carry

    def edge_rows():
        lax.fori_loop(0, offsets, contribution, 0)
        edge = dot(chosen[height:, :], contrib[...])
        edge_out[...] = edge.astype(BF16).reshape(2, halo, width)
        edges.start()
        mixes.start()

    def own_rows(piece):
        rows = slice(piece * 128, (piece + 1) * 128)
        local[rows] = dot(chosen[rows, :], contrib[...])

    def take_mixed():
        mixes.wait_recv()
        mixed[...] = dot(mix_in[...].reshape(slots, width), to_slots, 0, 0).T.astype(BF16)

    def finish():
        edges.wait()
        returned = edge_in[...].reshape(2 * halo, width)
        grad_features[...] = (local[...] + dot(border, returned)).astype(BF16)

    work = [edge_rows]
    work += [functools.partial(own_rows, piece) for piece in range(height // 128)]
    work += [take_mixed, finish]

    for b in range(bits):
        copy, at, length = halving(b, at, length, offset)
        places.append((at, length))
        if work:
            work.pop(0)()
        copy.wait()
        partial[pl.ds(at, length)] += half_in[offset : offset + length].astype(F32)
        offset += length
    summed[pl.ds(at, length)] = (partial[pl.ds(at, length)] * factor).astype(BF16)
    for b in reversed(range(bits)):
        at, length = places[b]
        copy = doubling(b, at, length)
        if work:
            work.pop(0)()
        copy.wait()
    for task in work:
        task()
    gathered_grads[...] = summed[...]
    for other in (cots, acts, backs, mixes):
        other.wait_send()


def shape(dims, kind):
    return jax.ShapeDtypeStruct(dims, kind)


def body(
    features, conv_weight, in_projection, out_projection, head_scale,
    neighbours, send_rows, send_count, window_slot, cotangent,
):
    height, width = features.shape
    halo = send_rows.shape[1]
    offsets = neighbours.shape[0]
    devices = lax.axis_size("bricks")
    capacity = height // devices + height // devices // 2
    cap = -(-capacity // 16) * 16
    slots = devices * cap
    parts = in_projection.shape[1] // width
    live = (offsets + parts + 1) * width
    total_rows = -(-live // (16 * devices)) * 16 * devices
    bits = devices.bit_length() - 1
    factor = (height * devices) ** (-0.5)
    rows = pltpu.VMEM((devices, cap, width), BF16)
    marked = pltpu.VMEM((devices, cap + 16, width), BF16)
    pair = pltpu.VMEM((2, halo, width), BF16)
    mixed, grad_features, grads = pl.pallas_call(
        functools.partial(level_kernel, devices, cap, halo, total_rows, factor),
        out_shape=(
            shape((height, width), BF16),
            shape((height, width), BF16),
            shape((total_rows, width), BF16),
        ),
        in_specs=[VMEM] * 8 + [SMEM] * 2,
        out_specs=[VMEM] * 3,
        scratch_shapes=[
            pltpu.VMEM((devices, 16, 128), F32),
            pltpu.VMEM((height + 2 * halo, offsets * height), BF16),
            pltpu.VMEM((offsets * width, height), BF16),
            pltpu.VMEM((offsets * height, width), BF16),
            pltpu.VMEM((width, height), F32),
            pltpu.VMEM((height, width), F32),
            pltpu.VMEM((total_rows, width), F32),
            pltpu.VMEM((total_rows, width), BF16),
            marked, marked, rows, rows, rows, rows, rows, rows,
            pair, pair, pair, pair,
            pltpu.VMEM((total_rows, width), BF16),
            pltpu.VMEM((total_rows, width), BF16),
            pltpu.SemaphoreType.DMA((8,)),
            pltpu.SemaphoreType.DMA((4,)),
            pltpu.SemaphoreType.DMA((4,)),
            pltpu.SemaphoreType.DMA((2 * bits,)),
            pltpu.SemaphoreType.DMA((2 * bits,)),
        ],
        compiler_params=pltpu.CompilerParams(
            collective_id=0, has_side_effects=True, vmem_limit_bytes=56 * 1024 * 1024
        ),
    )(
        features,
        conv_weight.reshape(offsets * width, width),
        in_projection,
        out_projection,
        neighbours,
        send_rows.reshape(1, 2 * halo),
        window_slot.reshape(1, height),
        cotangent,
        head_scale,
        send_count,
    )
    grads = grads.astype(F32).reshape(-1, width, width)
    grad_in = grads[offsets : offsets + parts].transpose(1, 0, 2).reshape(in_projection.shape)
    return (mixed, grad_features, grads[:offsets], grad_in, grads[offsets + parts])


def solution(mesh):
    return jax.shard_map(
        body,
        mesh=mesh,
        in_specs=(
            P(("groups", "bricks"), None),
            P(),
            P(),
            P(),
            P(),
            P(None, ("groups", "bricks")),
            P(("groups", "bricks"), None),
            P(("groups", "bricks")),
            P(("groups", "bricks")),
            P(("groups", "bricks"), None),
        ),
        out_specs=(
            P(("groups", "bricks"), None),
            P(("groups", "bricks"), None),
            P("groups", None, None),
            P("groups", None),
            P("groups", None),
        ),
        check_vma=False,
    )
```

```python
import functools

import jax
import jax.numpy as jnp
from jax import lax
from jax.experimental import pallas as pl
from jax.experimental.pallas import tpu as pltpu
from jax.sharding import PartitionSpec as P

HEADS = 2
EPS = 1e-06
F32 = jnp.float32
BF16 = jnp.bfloat16
VMEM = pl.BlockSpec(memory_space=pltpu.VMEM)
CHAINS = 4
SMEM = pl.BlockSpec(memory_space=pltpu.SMEM)


def dot(a, b, ca=1, cb=0):
    return lax.dot_general(a, b, (((ca,), (cb,)), ((), ())), preferred_element_type=F32)


def iota(shape, dim):
    return lax.broadcasted_iota(jnp.int32, shape, dim)


def select_rows(rows, lane_index):
    shape = (rows, lane_index.shape[1])
    return jnp.where(iota(shape, 0) == lane_index, 1.0, 0.0).astype(BF16)


def rank_plan(slot, devices, cap):
    height = slot.shape[1]
    bits = height.bit_length() - 1
    target = lax.shift_right_logical(slot, jnp.full_like(slot, bits))
    within = slot & (height - 1)
    member = iota((devices, height), 0) == target
    before = jnp.where(iota((height, height), 0) < iota((height, height), 1), 1.0, 0.0).astype(BF16)
    ones = jnp.where(member, 1.0, 0.0)
    counts = dot(ones.astype(BF16), before)
    rank = jnp.sum(counts * ones, axis=0, keepdims=True).astype(jnp.int32)
    return target, within, rank, target * cap + rank


def position_rows(target, within, rank, me, devices, cap):
    slots = devices * cap
    height = target.shape[1]
    where_to = select_rows(slots, rank + me * cap)
    shown = within + 1
    hit = iota((devices, height), 0) == target
    high = jnp.where(hit, lax.shift_right_logical(shown, jnp.full_like(shown, 8)), 0)
    low = jnp.where(hit, shown & 255, 0)
    return (
        dot(high.astype(F32).astype(BF16), where_to, 1, 1),
        dot(low.astype(F32).astype(BF16), where_to, 1, 1),
    )


def border_select(send, count0, count1, height):
    both = send.shape[1]
    lane = iota((1, both), 1)
    limit = jnp.where(lane < both // 2, count0, count1 + both // 2)
    return select_rows(height, jnp.where(lane < limit, send, -1))


def heads_forward(projected, scale):
    width = projected.shape[0] // 3
    dim = width // HEADS
    kept = []
    for h in range(HEADS):
        q = projected[h * dim : (h + 1) * dim]
        k = projected[width + h * dim : width + (h + 1) * dim]
        v = projected[2 * width + h * dim : 2 * width + (h + 1) * dim].astype(BF16)
        rq = lax.rsqrt(jnp.sum(q * q, axis=0, keepdims=True) + EPS)
        rk = lax.rsqrt(jnp.sum(k * k, axis=0, keepdims=True) + EPS)
        qp = (q * rq * scale[h]).astype(BF16)
        kp = (k * rk).astype(BF16)
        e = jnp.exp(dot(kp, qp, 0, 0))
        p = e * (1.0 / jnp.sum(e, axis=0, keepdims=True))
        w = p.astype(BF16)
        kept.append((q, k, v, rq, rk, qp, kp, p, w, dot(v, w).astype(BF16)))
    return kept


def heads_backward(kept, grad_core, scale):
    grads = [[], [], []]
    for h in range(HEADS):
        q, k, v, rq, rk, qp, kp, p, w, _ = kept[h]
        dim = q.shape[0]
        grad_h = grad_core[h * dim : (h + 1) * dim]
        dw = dot(v, grad_h, 0, 0).astype(BF16).astype(F32)
        dv = dot(grad_h, w, 1, 1)
        ds = (p * (dw - jnp.sum(dw * p, axis=0, keepdims=True))).astype(BF16)
        dqp = dot(kp, ds).astype(BF16).astype(F32)
        dkp = dot(qp, ds, 1, 1).astype(BF16).astype(F32)
        dq = scale[h] * rq * (dqp - q * (rq * rq) * jnp.sum(dqp * q, axis=0, keepdims=True))
        dk = rk * (dkp - k * (rk * rk) * jnp.sum(dkp * k, axis=0, keepdims=True))
        grads[0].append(dq.astype(BF16))
        grads[1].append(dk.astype(BF16))
        grads[2].append(dv.astype(BF16))
    return jnp.concatenate(grads[0] + grads[1] + grads[2], axis=0)


class Exchange:
    def __init__(self, devices, me, out, into, sems, which):
        self.devices, self.me, self.out, self.into = devices, me, out, into
        self.send, self.recv = sems.at[2 * which], sems.at[2 * which + 1]

    def start(self):
        def step(s, carry):
            to = lax.rem(self.me + s, self.devices)
            pltpu.make_async_remote_copy(
                src_ref=self.out.at[to],
                dst_ref=self.into.at[self.me],
                send_sem=self.send,
                recv_sem=self.recv,
                device_id={"bricks": to},
                device_id_type=pl.DeviceIdType.MESH,
            ).start()
            return carry

        lax.fori_loop(1, self.devices, step, 0)
        self.into[self.me] = self.out[self.me]

    def wait_recv(self):
        part = self.into.at[pl.ds(0, self.devices - 1)]
        pltpu.make_async_copy(part, part, self.recv).wait()

    def wait_send(self):
        part = self.out.at[pl.ds(0, self.devices - 1)]
        pltpu.make_async_copy(part, part, self.send).wait()


class Edges:
    def __init__(self, devices, me, out, into, sems):
        self.has = (me > 0, me < devices - 1)
        self.into = into
        self.copies = [
            pltpu.make_async_remote_copy(
                src_ref=out.at[side],
                dst_ref=into.at[1 - side],
                send_sem=sems.at[side],
                recv_sem=sems.at[2 + 1 - side],
                device_id={"bricks": lax.rem(me + step + devices, devices)},
                device_id_type=pl.DeviceIdType.MESH,
            )
            for side, step in ((0, -1), (1, 1))
        ]

    def blank(self):
        for side in range(2):
            @pl.when(jnp.logical_not(self.has[side]))
            def _():
                self.into[side] = jnp.zeros(self.into.shape[1:], self.into.dtype)

    def start(self):
        for side in range(2):
            @pl.when(self.has[side])
            def _():
                self.copies[side].start()

    def wait(self):
        for side in range(2):
            @pl.when(self.has[side])
            def _():
                self.copies[side].wait_send()
                self.copies[1 - side].wait_recv()


class Chain:
    def __init__(self, at, length, order):
        self.at, self.length, self.offset, self.order = at, length, at, order
        self.places = []


def finish_kernel(mixed, features, grads, *outs):
    offsets = outs[2].shape[0]
    width = mixed.shape[1]
    outs[0][...] = mixed[...]
    outs[1][...] = features[...]
    outs[2][...] = grads[: offsets * width].astype(F32).reshape(outs[2].shape)
    base = offsets * width
    for j in range(outs[3].shape[1] // width):
        outs[3][:, j * width : (j + 1) * width] = grads[base : base + width].astype(F32)
        base += width
    outs[4][...] = grads[base : base + width].astype(F32)


def level_kernel(
    devices, cap, halo, total_rows, factor,
    feat, weight, in_proj, out_proj, near, send, slot, cot, scale, count,
    mixed, grad_features, gathered_grads,
    stage, chosen, gathered, contrib, filtered, local, partial, summed,
    cot_out, cot_in, act_out, act_in, back_out, back_in, mix_out, mix_in,
    halo_out, halo_in, edge_out, edge_in, half_out, half_in,
    sems, halo_sems, edge_sems, half_sems, full_sems,
):
    me = lax.axis_index("bricks")
    height, width = feat.shape
    offsets = near.shape[0]
    slots = devices * cap
    chunks = slots // 128
    table_rows = height + 2 * halo
    barrier = pltpu.get_barrier_semaphore()
    halos = Edges(devices, me, halo_out, halo_in, halo_sems)
    edges = Edges(devices, me, edge_out, edge_in, edge_sems)
    halos.blank()
    edges.blank()

    def greet(s, carry):
        pl.semaphore_signal(
            barrier,
            inc=1,
            device_id={"bricks": lax.rem(me + s, devices)},
            device_id_type=pl.DeviceIdType.MESH,
        )
        return carry

    lax.fori_loop(1, devices, greet, 0)
    cots = Exchange(devices, me, cot_out, cot_in, sems, 0)
    acts = Exchange(devices, me, act_out, act_in, sems, 1)
    backs = Exchange(devices, me, back_out, back_in, sems, 2)
    mixes = Exchange(devices, me, mix_out, mix_in, sems, 3)

    border = border_select(send[...], count[0], count[1], height)
    halo_out[...] = dot(border, feat[...], 0, 0).astype(BF16).reshape(2, halo, width)
    pl.semaphore_wait(barrier, devices - 1)
    halos.start()

    target, within, rank, placing = rank_plan(slot[...], devices, cap)
    to_slots = select_rows(slots, placing)
    cot_out[:, :cap, :] = dot(to_slots, cot[...]).astype(BF16).reshape(devices, cap, width)
    high, low = position_rows(target, within, rank, me, devices, cap)
    stage[...] = jnp.zeros_like(stage)
    for r in range(chunks):
        stage[:, r, :] = high[:, r * 128 : (r + 1) * 128]
        stage[:, chunks + r, :] = low[:, r * 128 : (r + 1) * 128]
    cot_out[:, cap:, :] = stage[...].astype(BF16)
    cots.start()

    def choose(k, carry):
        at = pl.ds(pl.multiple_of(k * height, height), height)
        chosen[:, at] = select_rows(table_rows, near[pl.ds(k, 1), :])
        return carry

    lax.fori_loop(0, offsets, choose, 0)
    halos.wait()
    table = jnp.concatenate(
        [feat[...].astype(F32).T, halo_in[...].reshape(2 * halo, width).astype(F32).T], axis=1
    ).astype(BF16)

    def gather(k, carry):
        at = pl.ds(pl.multiple_of(k * height, height), height)
        rows = pl.ds(pl.multiple_of(k * width, width), width)
        gathered[rows, :] = dot(table, chosen[:, at]).astype(BF16)
        return carry

    lax.fori_loop(0, offsets, gather, 0)
    total = dot(weight[...], gathered[...], 0, 0)
    filtered[...] = total
    activated = (total * jax.nn.sigmoid(total)).astype(BF16)
    act_out[...] = dot(to_slots, activated, 1, 1).astype(BF16).reshape(devices, cap, width)
    acts.start()

    cots.wait_recv()
    marks = jnp.sum(cot_in[:, cap:, :].astype(F32), axis=0)
    landing = jnp.concatenate(
        [marks[r : r + 1] * 256.0 + marks[chunks + r : chunks + r + 1] for r in range(chunks)], axis=1
    ).astype(jnp.int32) - 1
    to_window = select_rows(height, landing)
    grad_win = dot(to_window, cot_in[:, :cap, :].reshape(slots, width)).astype(BF16)
    grad_core = dot(out_proj[...], grad_win, 1, 1).astype(BF16)
    scales = (scale[0], scale[1])
    acts.wait_recv()
    win = dot(to_window, act_in[...].reshape(slots, width)).astype(BF16)
    projected = dot(in_proj[...], win, 0, 1).astype(BF16).astype(F32)
    kept = heads_forward(projected, scales)
    grad_projected = heads_backward(kept, grad_core, scales)
    grad_back = dot(in_proj[...], grad_projected).astype(BF16)
    back_out[...] = dot(grad_back, to_window).T.astype(BF16).reshape(devices, cap, width)
    backs.start()
    core = jnp.concatenate([kept[h][-1] for h in range(HEADS)], axis=0)
    mixed_win = dot(out_proj[...], core, 0, 0).astype(BF16)
    mix_out[...] = dot(mixed_win, to_window).T.astype(BF16).reshape(devices, cap, width)
    base = offsets * width
    grad_in = dot(win, grad_projected, 0, 1)
    parts = in_proj.shape[1] // width
    for j in range(parts):
        partial[base + j * width : base + (j + 1) * width] = grad_in[:, j * width : (j + 1) * width]
    base += parts * width
    partial[base : base + width] = dot(core, grad_win)
    base += width
    partial[base:] = jnp.zeros((total_rows - base, width), F32)

    f = filtered[...]
    sigmoid = jax.nn.sigmoid(f)
    slope = sigmoid * (1.0 + f * (1.0 - sigmoid))
    backs.wait_recv()
    grad_act = dot(back_in[...].reshape(slots, width), to_slots, 0, 0)
    grad = (grad_act * slope).T.astype(BF16)
    partial[: offsets * width] = dot(gathered[...], grad)

    bits = devices.bit_length() - 1
    orders = (list(range(bits)), list(range(1)) + list(range(2, bits)) + list(range(1, min(2, bits))))
    share = total_rows // CHAINS
    chains = [Chain(c * share, share, orders[c % 2]) for c in range(CHAINS)]

    def halving(c, i):
        chain = chains[c]
        b = chain.order[i]
        length = chain.length // 2
        bit = lax.rem(me // (1 << b), 2)
        other = me + (1 - 2 * bit) * (1 << b)
        keep = pl.multiple_of(chain.at + bit * length, 16)
        give = pl.multiple_of(chain.at + (1 - bit) * length, 16)
        part = pl.ds(chain.offset, length)
        half_out[part] = partial[pl.ds(give, length)].astype(BF16)
        chain.copy = pltpu.make_async_remote_copy(
            src_ref=half_out.at[part],
            dst_ref=half_in.at[part],
            send_sem=half_sems.at[2 * (c * bits + i)],
            recv_sem=half_sems.at[2 * (c * bits + i) + 1],
            device_id={"bricks": other},
            device_id_type=pl.DeviceIdType.MESH,
        )
        chain.copy.start()
        chain.at, chain.length = keep, length
        chain.places.append((keep, length))

    def add_half(c):
        chain = chains[c]
        chain.copy.wait()
        partial[pl.ds(chain.at, chain.length)] += half_in[
            pl.ds(chain.offset, chain.length)
        ].astype(F32)
        chain.offset += chain.length

    def doubling(c, i):
        chain = chains[c]
        b = chain.order[i]
        at, length = chain.places[i]
        bit = lax.rem(me // (1 << b), 2)
        other = me + (1 - 2 * bit) * (1 << b)
        part = summed.at[pl.ds(pl.multiple_of(at, 16), length)]
        chain.copy = pltpu.make_async_remote_copy(
            src_ref=part,
            dst_ref=part,
            send_sem=full_sems.at[2 * (c * bits + i)],
            recv_sem=full_sems.at[2 * (c * bits + i) + 1],
            device_id={"bricks": other},
            device_id_type=pl.DeviceIdType.MESH,
        )
        chain.copy.start()

    def contribution(k, carry):
        rows = pl.ds(pl.multiple_of(k * height, height), height)
        taps = pl.ds(pl.multiple_of(k * width, width), width)
        contrib[rows, :] = dot(grad, weight[taps, :], 1, 1).astype(BF16)
        return carry

    def edge_rows():
        lax.fori_loop(0, offsets, contribution, 0)
        edge = dot(chosen[height:, :], contrib[...])
        edge_out[...] = edge.astype(BF16).reshape(2, halo, width)
        edges.start()
        mixes.start()

    def own_rows(piece):
        rows = slice(piece * 128, (piece + 1) * 128)
        local[rows] = dot(chosen[rows, :], contrib[...])

    def take_mixed():
        mixes.wait_recv()
        mixed[...] = dot(mix_in[...].reshape(slots, width), to_slots, 0, 0).T.astype(BF16)

    def finish():
        edges.wait()
        returned = edge_in[...].reshape(2 * halo, width)
        grad_features[...] = (local[...] + dot(border, returned)).astype(BF16)

    work = [edge_rows]
    work += [functools.partial(own_rows, piece) for piece in range(height // 128)]
    work += [take_mixed, finish]

    for c in range(CHAINS):
        halving(c, 0)
    for i in range(bits):
        if work:
            work.pop(0)()
        for c in range(CHAINS):
            add_half(c)
            if i + 1 < bits:
                halving(c, i + 1)
            else:
                done = pl.ds(chains[c].at, chains[c].length)
                summed[done] = (partial[done] * factor).astype(BF16)
                doubling(c, bits - 1)
    for i in reversed(range(bits)):
        if work:
            work.pop(0)()
        for c in range(CHAINS):
            chains[c].copy.wait()
            if i:
                doubling(c, i - 1)
    for task in work:
        task()
    gathered_grads[...] = summed[...]
    for other in (cots, acts, backs, mixes):
        other.wait_send()


def shape(dims, kind):
    return jax.ShapeDtypeStruct(dims, kind)


def body(
    features, conv_weight, in_projection, out_projection, head_scale,
    neighbours, send_rows, send_count, window_slot, cotangent,
):
    height, width = features.shape
    halo = send_rows.shape[1]
    offsets = neighbours.shape[0]
    devices = lax.axis_size("bricks")
    capacity = height // devices + height // devices // 2
    cap = -(-capacity // 16) * 16
    slots = devices * cap
    parts = in_projection.shape[1] // width
    live = (offsets + parts + 1) * width
    total_rows = -(-live // (16 * devices * CHAINS)) * 16 * devices * CHAINS
    bits = devices.bit_length() - 1
    factor = (height * devices) ** (-0.5)
    rows = pltpu.VMEM((devices, cap, width), BF16)
    marked = pltpu.VMEM((devices, cap + 16, width), BF16)
    pair = pltpu.VMEM((2, halo, width), BF16)
    mixed, grad_features, grads = pl.pallas_call(
        functools.partial(level_kernel, devices, cap, halo, total_rows, factor),
        out_shape=(
            shape((height, width), BF16),
            shape((height, width), BF16),
            shape((total_rows, width), BF16),
        ),
        in_specs=[VMEM] * 8 + [SMEM] * 2,
        out_specs=[VMEM] * 3,
        scratch_shapes=[
            pltpu.VMEM((devices, 16, 128), F32),
            pltpu.VMEM((height + 2 * halo, offsets * height), BF16),
            pltpu.VMEM((offsets * width, height), BF16),
            pltpu.VMEM((offsets * height, width), BF16),
            pltpu.VMEM((width, height), F32),
            pltpu.VMEM((height, width), F32),
            pltpu.VMEM((total_rows, width), F32),
            pltpu.VMEM((total_rows, width), BF16),
            marked, marked, rows, rows, rows, rows, rows, rows,
            pair, pair, pair, pair,
            pltpu.VMEM((total_rows, width), BF16),
            pltpu.VMEM((total_rows, width), BF16),
            pltpu.SemaphoreType.DMA((8,)),
            pltpu.SemaphoreType.DMA((4,)),
            pltpu.SemaphoreType.DMA((4,)),
            pltpu.SemaphoreType.DMA((2 * bits * CHAINS,)),
            pltpu.SemaphoreType.DMA((2 * bits * CHAINS,)),
        ],
        compiler_params=pltpu.CompilerParams(
            collective_id=0, has_side_effects=True, vmem_limit_bytes=56 * 1024 * 1024
        ),
    )(
        features,
        conv_weight.reshape(offsets * width, width),
        in_projection,
        out_projection,
        neighbours,
        send_rows.reshape(1, 2 * halo),
        window_slot.reshape(1, height),
        cotangent,
        head_scale,
        send_count,
    )
    return tuple(
        pl.pallas_call(
            finish_kernel,
            out_shape=(
                shape((height, width), BF16),
                shape((height, width), BF16),
                shape(conv_weight.shape, F32),
                shape(in_projection.shape, F32),
                shape(out_projection.shape, F32),
            ),
            in_specs=[VMEM] * 3,
            out_specs=[VMEM] * 5,
            compiler_params=pltpu.CompilerParams(vmem_limit_bytes=32 * 1024 * 1024),
        )(mixed, grad_features, grads)
    )


def solution(mesh):
    return jax.shard_map(
        body,
        mesh=mesh,
        in_specs=(
            P(("groups", "bricks"), None),
            P(),
            P(),
            P(),
            P(),
            P(None, ("groups", "bricks")),
            P(("groups", "bricks"), None),
            P(("groups", "bricks")),
            P(("groups", "bricks")),
            P(("groups", "bricks"), None),
        ),
        out_specs=(
            P(("groups", "bricks"), None),
            P(("groups", "bricks"), None),
            P("groups", None, None),
            P("groups", None),
            P("groups", None),
        ),
        check_vma=False,
    )
```

```python
import functools

import jax
import jax.numpy as jnp
from jax import lax
from jax.experimental import pallas as pl
from jax.experimental.pallas import tpu as pltpu
from jax.sharding import PartitionSpec as P

HEADS = 2
EPS = 1e-06
F32 = jnp.float32
BF16 = jnp.bfloat16
VMEM = pl.BlockSpec(memory_space=pltpu.VMEM)
CHAINS = 4
SMEM = pl.BlockSpec(memory_space=pltpu.SMEM)


def dot(a, b, ca=1, cb=0):
    return lax.dot_general(a, b, (((ca,), (cb,)), ((), ())), preferred_element_type=F32)


def iota(shape, dim):
    return lax.broadcasted_iota(jnp.int32, shape, dim)


def select_rows(rows, lane_index):
    shape = (rows, lane_index.shape[1])
    return jnp.where(iota(shape, 0) == lane_index, 1.0, 0.0).astype(BF16)


def rank_plan(slot, devices, cap):
    height = slot.shape[1]
    bits = height.bit_length() - 1
    target = lax.shift_right_logical(slot, jnp.full_like(slot, bits))
    within = slot & (height - 1)
    member = iota((devices, height), 0) == target
    before = jnp.where(iota((height, height), 0) < iota((height, height), 1), 1.0, 0.0).astype(BF16)
    ones = jnp.where(member, 1.0, 0.0)
    counts = dot(ones.astype(BF16), before)
    rank = jnp.sum(counts * ones, axis=0, keepdims=True).astype(jnp.int32)
    return target, within, rank, target * cap + rank


def position_rows(target, within, rank, me, devices, cap):
    slots = devices * cap
    height = target.shape[1]
    where_to = select_rows(slots, rank + me * cap)
    shown = within + 1
    hit = iota((devices, height), 0) == target
    high = jnp.where(hit, lax.shift_right_logical(shown, jnp.full_like(shown, 8)), 0)
    low = jnp.where(hit, shown & 255, 0)
    return (
        dot(high.astype(F32).astype(BF16), where_to, 1, 1),
        dot(low.astype(F32).astype(BF16), where_to, 1, 1),
    )


def border_select(send, count0, count1, height):
    both = send.shape[1]
    lane = iota((1, both), 1)
    limit = jnp.where(lane < both // 2, count0, count1 + both // 2)
    return select_rows(height, jnp.where(lane < limit, send, -1))


def heads_forward(projected, scale):
    width = projected.shape[0] // 3
    dim = width // HEADS
    kept = []
    for h in range(HEADS):
        q = projected[h * dim : (h + 1) * dim]
        k = projected[width + h * dim : width + (h + 1) * dim]
        v = projected[2 * width + h * dim : 2 * width + (h + 1) * dim].astype(BF16)
        rq = lax.rsqrt(jnp.sum(q * q, axis=0, keepdims=True) + EPS)
        rk = lax.rsqrt(jnp.sum(k * k, axis=0, keepdims=True) + EPS)
        qp = (q * rq * scale[h]).astype(BF16)
        kp = (k * rk).astype(BF16)
        e = jnp.exp(dot(kp, qp, 0, 0))
        p = e * (1.0 / jnp.sum(e, axis=0, keepdims=True))
        w = p.astype(BF16)
        kept.append((q, k, v, rq, rk, qp, kp, p, w, dot(v, w).astype(BF16)))
    return kept


def heads_backward(kept, grad_core, scale):
    grads = [[], [], []]
    for h in range(HEADS):
        q, k, v, rq, rk, qp, kp, p, w, _ = kept[h]
        dim = q.shape[0]
        grad_h = grad_core[h * dim : (h + 1) * dim]
        dw = dot(v, grad_h, 0, 0).astype(BF16).astype(F32)
        dv = dot(grad_h, w, 1, 1)
        ds = (p * (dw - jnp.sum(dw * p, axis=0, keepdims=True))).astype(BF16)
        dqp = dot(kp, ds).astype(BF16).astype(F32)
        dkp = dot(qp, ds, 1, 1).astype(BF16).astype(F32)
        dq = scale[h] * rq * (dqp - q * (rq * rq) * jnp.sum(dqp * q, axis=0, keepdims=True))
        dk = rk * (dkp - k * (rk * rk) * jnp.sum(dkp * k, axis=0, keepdims=True))
        grads[0].append(dq.astype(BF16))
        grads[1].append(dk.astype(BF16))
        grads[2].append(dv.astype(BF16))
    return jnp.concatenate(grads[0] + grads[1] + grads[2], axis=0)


class Exchange:
    def __init__(self, devices, me, out, into, sems, which):
        self.devices, self.me, self.out, self.into = devices, me, out, into
        self.send, self.recv = sems.at[2 * which], sems.at[2 * which + 1]

    def start(self):
        def step(s, carry):
            to = lax.rem(self.me + s, self.devices)
            pltpu.make_async_remote_copy(
                src_ref=self.out.at[to],
                dst_ref=self.into.at[self.me],
                send_sem=self.send,
                recv_sem=self.recv,
                device_id={"bricks": to},
                device_id_type=pl.DeviceIdType.MESH,
            ).start()
            return carry

        lax.fori_loop(1, self.devices, step, 0)
        self.into[self.me] = self.out[self.me]

    def wait_recv(self):
        part = self.into.at[pl.ds(0, self.devices - 1)]
        pltpu.make_async_copy(part, part, self.recv).wait()

    def wait_send(self):
        part = self.out.at[pl.ds(0, self.devices - 1)]
        pltpu.make_async_copy(part, part, self.send).wait()


class Edges:
    def __init__(self, devices, me, out, into, sems):
        self.has = (me > 0, me < devices - 1)
        self.into = into
        self.copies = [
            pltpu.make_async_remote_copy(
                src_ref=out.at[side],
                dst_ref=into.at[1 - side],
                send_sem=sems.at[side],
                recv_sem=sems.at[2 + 1 - side],
                device_id={"bricks": lax.rem(me + step + devices, devices)},
                device_id_type=pl.DeviceIdType.MESH,
            )
            for side, step in ((0, -1), (1, 1))
        ]

    def blank(self):
        for side in range(2):
            @pl.when(jnp.logical_not(self.has[side]))
            def _():
                self.into[side] = jnp.zeros(self.into.shape[1:], self.into.dtype)

    def start(self):
        for side in range(2):
            @pl.when(self.has[side])
            def _():
                self.copies[side].start()

    def wait(self):
        for side in range(2):
            @pl.when(self.has[side])
            def _():
                self.copies[side].wait_send()
                self.copies[1 - side].wait_recv()


class Chain:
    def __init__(self, at, length, order):
        self.at, self.length, self.offset, self.order = at, length, at, order
        self.places = []


def finish_kernel(result, *outs):
    offsets = outs[2].shape[0]
    height, width = outs[0].shape
    outs[0][...] = result[:height]
    outs[1][...] = result[height : 2 * height]
    base = 2 * height + offsets * width
    outs[2][...] = result[2 * height : base].astype(F32).reshape(outs[2].shape)
    for j in range(outs[3].shape[1] // width):
        outs[3][:, j * width : (j + 1) * width] = result[base : base + width].astype(F32)
        base += width
    outs[4][...] = result[base : base + width].astype(F32)


def level_kernel(
    devices, cap, halo, total_rows, factor,
    feat, weight_hbm, in_proj, out_proj, near, send, slot, cot, scale, count,
    result,
    weight, weight_sem, stage, chosen, gathered, contrib, filtered, local, partial, summed,
    cot_out, cot_in, act_out, act_in, back_out, back_in, mix_out, mix_in,
    halo_out, halo_in, edge_out, edge_in, half_out, half_in,
    sems, halo_sems, edge_sems, half_sems, full_sems,
):
    me = lax.axis_index("bricks")
    height, width = feat.shape
    offsets = near.shape[0]
    slots = devices * cap
    chunks = slots // 128
    table_rows = height + 2 * halo
    barrier = pltpu.get_barrier_semaphore()
    halos = Edges(devices, me, halo_out, halo_in, halo_sems)
    edges = Edges(devices, me, edge_out, edge_in, edge_sems)
    load = pltpu.make_async_copy(weight_hbm, weight, weight_sem)
    load.start()
    halos.blank()
    edges.blank()

    def greet(s, carry):
        pl.semaphore_signal(
            barrier,
            inc=1,
            device_id={"bricks": lax.rem(me + s, devices)},
            device_id_type=pl.DeviceIdType.MESH,
        )
        return carry

    lax.fori_loop(1, devices, greet, 0)
    cots = Exchange(devices, me, cot_out, cot_in, sems, 0)
    acts = Exchange(devices, me, act_out, act_in, sems, 1)
    backs = Exchange(devices, me, back_out, back_in, sems, 2)
    mixes = Exchange(devices, me, mix_out, mix_in, sems, 3)

    border = border_select(send[...], count[0], count[1], height)
    halo_out[...] = dot(border, feat[...], 0, 0).astype(BF16).reshape(2, halo, width)
    pl.semaphore_wait(barrier, devices - 1)
    halos.start()

    target, within, rank, placing = rank_plan(slot[...], devices, cap)
    to_slots = select_rows(slots, placing)
    cot_out[:, :cap, :] = dot(to_slots, cot[...]).astype(BF16).reshape(devices, cap, width)
    high, low = position_rows(target, within, rank, me, devices, cap)
    stage[...] = jnp.zeros_like(stage)
    for r in range(chunks):
        stage[:, r, :] = high[:, r * 128 : (r + 1) * 128]
        stage[:, chunks + r, :] = low[:, r * 128 : (r + 1) * 128]
    cot_out[:, cap:, :] = stage[...].astype(BF16)
    cots.start()

    def choose(k, carry):
        at = pl.ds(pl.multiple_of(k * height, height), height)
        chosen[:, at] = select_rows(table_rows, near[pl.ds(k, 1), :])
        return carry

    lax.fori_loop(0, offsets, choose, 0)
    halos.wait()
    table = jnp.concatenate(
        [feat[...].astype(F32).T, halo_in[...].reshape(2 * halo, width).astype(F32).T], axis=1
    ).astype(BF16)

    def gather(k, carry):
        at = pl.ds(pl.multiple_of(k * height, height), height)
        rows = pl.ds(pl.multiple_of(k * width, width), width)
        gathered[rows, :] = dot(table, chosen[:, at]).astype(BF16)
        return carry

    lax.fori_loop(0, offsets, gather, 0)
    load.wait()
    total = dot(weight[...], gathered[...], 0, 0)
    filtered[...] = total
    activated = (total * jax.nn.sigmoid(total)).astype(BF16)
    act_out[...] = dot(to_slots, activated, 1, 1).astype(BF16).reshape(devices, cap, width)
    acts.start()

    cots.wait_recv()
    marks = jnp.sum(cot_in[:, cap:, :].astype(F32), axis=0)
    landing = jnp.concatenate(
        [marks[r : r + 1] * 256.0 + marks[chunks + r : chunks + r + 1] for r in range(chunks)], axis=1
    ).astype(jnp.int32) - 1
    to_window = select_rows(height, landing)
    grad_win = dot(to_window, cot_in[:, :cap, :].reshape(slots, width)).astype(BF16)
    grad_core = dot(out_proj[...], grad_win, 1, 1).astype(BF16)
    scales = (scale[0], scale[1])
    acts.wait_recv()
    win = dot(to_window, act_in[...].reshape(slots, width)).astype(BF16)
    projected = dot(in_proj[...], win, 0, 1).astype(BF16).astype(F32)
    kept = heads_forward(projected, scales)
    grad_projected = heads_backward(kept, grad_core, scales)
    grad_back = dot(in_proj[...], grad_projected).astype(BF16)
    back_out[...] = dot(grad_back, to_window).T.astype(BF16).reshape(devices, cap, width)
    backs.start()
    core = jnp.concatenate([kept[h][-1] for h in range(HEADS)], axis=0)
    mixed_win = dot(out_proj[...], core, 0, 0).astype(BF16)
    mix_out[...] = dot(mixed_win, to_window).T.astype(BF16).reshape(devices, cap, width)
    base = offsets * width
    grad_in = dot(win, grad_projected, 0, 1)
    parts = in_proj.shape[1] // width
    for j in range(parts):
        partial[base + j * width : base + (j + 1) * width] = grad_in[:, j * width : (j + 1) * width]
    base += parts * width
    partial[base : base + width] = dot(core, grad_win)
    base += width
    partial[base:] = jnp.zeros((total_rows - base, width), F32)

    f = filtered[...]
    sigmoid = jax.nn.sigmoid(f)
    slope = sigmoid * (1.0 + f * (1.0 - sigmoid))
    backs.wait_recv()
    grad_act = dot(back_in[...].reshape(slots, width), to_slots, 0, 0)
    grad = (grad_act * slope).T.astype(BF16)
    partial[: offsets * width] = dot(gathered[...], grad)

    bits = devices.bit_length() - 1
    orders = (list(range(bits)), list(range(1)) + list(range(2, bits)) + list(range(1, min(2, bits))))
    share = total_rows // CHAINS
    chains = [Chain(c * share, share, orders[c % 2]) for c in range(CHAINS)]

    def halving(c, i):
        chain = chains[c]
        b = chain.order[i]
        length = chain.length // 2
        bit = lax.rem(me // (1 << b), 2)
        other = me + (1 - 2 * bit) * (1 << b)
        keep = pl.multiple_of(chain.at + bit * length, 16)
        give = pl.multiple_of(chain.at + (1 - bit) * length, 16)
        part = pl.ds(chain.offset, length)
        half_out[part] = partial[pl.ds(give, length)].astype(BF16)
        chain.copy = pltpu.make_async_remote_copy(
            src_ref=half_out.at[part],
            dst_ref=half_in.at[part],
            send_sem=half_sems.at[2 * (c * bits + i)],
            recv_sem=half_sems.at[2 * (c * bits + i) + 1],
            device_id={"bricks": other},
            device_id_type=pl.DeviceIdType.MESH,
        )
        chain.copy.start()
        chain.at, chain.length = keep, length
        chain.places.append((keep, length))

    def add_half(c):
        chain = chains[c]
        chain.copy.wait()
        partial[pl.ds(chain.at, chain.length)] += half_in[
            pl.ds(chain.offset, chain.length)
        ].astype(F32)
        chain.offset += chain.length

    def doubling(c, i):
        chain = chains[c]
        b = chain.order[i]
        at, length = chain.places[i]
        bit = lax.rem(me // (1 << b), 2)
        other = me + (1 - 2 * bit) * (1 << b)
        part = summed.at[pl.ds(pl.multiple_of(at, 16), length)]
        chain.copy = pltpu.make_async_remote_copy(
            src_ref=part,
            dst_ref=part,
            send_sem=full_sems.at[2 * (c * bits + i)],
            recv_sem=full_sems.at[2 * (c * bits + i) + 1],
            device_id={"bricks": other},
            device_id_type=pl.DeviceIdType.MESH,
        )
        chain.copy.start()

    def contribution(k, carry):
        rows = pl.ds(pl.multiple_of(k * height, height), height)
        taps = pl.ds(pl.multiple_of(k * width, width), width)
        contrib[rows, :] = dot(grad, weight[taps, :], 1, 1).astype(BF16)
        return carry

    def edge_rows():
        lax.fori_loop(0, offsets, contribution, 0)
        edge = dot(chosen[height:, :], contrib[...])
        edge_out[...] = edge.astype(BF16).reshape(2, halo, width)
        edges.start()
        mixes.start()

    def own_rows(piece):
        rows = slice(piece * 128, (piece + 1) * 128)
        local[rows] = dot(chosen[rows, :], contrib[...])

    def take_mixed():
        mixes.wait_recv()
        result[:height] = dot(mix_in[...].reshape(slots, width), to_slots, 0, 0).T.astype(BF16)

    def finish():
        edges.wait()
        returned = edge_in[...].reshape(2 * halo, width)
        result[height : 2 * height] = (local[...] + dot(border, returned)).astype(BF16)

    work = [edge_rows]
    work += [functools.partial(own_rows, piece) for piece in range(height // 128)]
    work += [take_mixed, finish]

    for c in range(CHAINS):
        halving(c, 0)
    for i in range(bits):
        if work:
            work.pop(0)()
        for c in range(CHAINS):
            add_half(c)
            if i + 1 < bits:
                halving(c, i + 1)
            else:
                done = pl.ds(chains[c].at, chains[c].length)
                summed[done] = (partial[done] * factor).astype(BF16)
                doubling(c, bits - 1)
    for i in reversed(range(bits)):
        if work:
            work.pop(0)()
        for c in range(CHAINS):
            chains[c].copy.wait()
            if i:
                doubling(c, i - 1)
    for task in work:
        task()
    result[2 * height :] = summed[...]
    for other in (cots, acts, backs, mixes):
        other.wait_send()


def shape(dims, kind):
    return jax.ShapeDtypeStruct(dims, kind)


def body(
    features, conv_weight, in_projection, out_projection, head_scale,
    neighbours, send_rows, send_count, window_slot, cotangent,
):
    height, width = features.shape
    halo = send_rows.shape[1]
    offsets = neighbours.shape[0]
    devices = lax.axis_size("bricks")
    capacity = height // devices + height // devices // 2
    cap = -(-capacity // 16) * 16
    slots = devices * cap
    parts = in_projection.shape[1] // width
    live = (offsets + parts + 1) * width
    total_rows = -(-live // (16 * devices * CHAINS)) * 16 * devices * CHAINS
    bits = devices.bit_length() - 1
    factor = (height * devices) ** (-0.5)
    rows = pltpu.VMEM((devices, cap, width), BF16)
    marked = pltpu.VMEM((devices, cap + 16, width), BF16)
    pair = pltpu.VMEM((2, halo, width), BF16)
    result = pl.pallas_call(
        functools.partial(level_kernel, devices, cap, halo, total_rows, factor),
        out_shape=shape((2 * height + total_rows, width), BF16),
        in_specs=[VMEM, pl.BlockSpec(memory_space=pl.ANY)] + [VMEM] * 6 + [SMEM] * 2,
        out_specs=VMEM,
        scratch_shapes=[
            pltpu.VMEM((offsets * width, width), BF16),
            pltpu.SemaphoreType.DMA,
            pltpu.VMEM((devices, 16, 128), F32),
            pltpu.VMEM((height + 2 * halo, offsets * height), BF16),
            pltpu.VMEM((offsets * width, height), BF16),
            pltpu.VMEM((offsets * height, width), BF16),
            pltpu.VMEM((width, height), F32),
            pltpu.VMEM((height, width), F32),
            pltpu.VMEM((total_rows, width), F32),
            pltpu.VMEM((total_rows, width), BF16),
            marked, marked, rows, rows, rows, rows, rows, rows,
            pair, pair, pair, pair,
            pltpu.VMEM((total_rows, width), BF16),
            pltpu.VMEM((total_rows, width), BF16),
            pltpu.SemaphoreType.DMA((8,)),
            pltpu.SemaphoreType.DMA((4,)),
            pltpu.SemaphoreType.DMA((4,)),
            pltpu.SemaphoreType.DMA((2 * bits * CHAINS,)),
            pltpu.SemaphoreType.DMA((2 * bits * CHAINS,)),
        ],
        compiler_params=pltpu.CompilerParams(
            collective_id=0, has_side_effects=True, vmem_limit_bytes=56 * 1024 * 1024
        ),
    )(
        features,
        conv_weight.reshape(offsets * width, width),
        in_projection,
        out_projection,
        neighbours,
        send_rows.reshape(1, 2 * halo),
        window_slot.reshape(1, height),
        cotangent,
        head_scale,
        send_count,
    )
    return tuple(
        pl.pallas_call(
            finish_kernel,
            out_shape=(
                shape((height, width), BF16),
                shape((height, width), BF16),
                shape(conv_weight.shape, F32),
                shape(in_projection.shape, F32),
                shape(out_projection.shape, F32),
            ),
            in_specs=[VMEM],
            out_specs=[VMEM] * 5,
            compiler_params=pltpu.CompilerParams(vmem_limit_bytes=32 * 1024 * 1024),
        )(result)
    )


def solution(mesh):
    return jax.shard_map(
        body,
        mesh=mesh,
        in_specs=(
            P(("groups", "bricks"), None),
            P(),
            P(),
            P(),
            P(),
            P(None, ("groups", "bricks")),
            P(("groups", "bricks"), None),
            P(("groups", "bricks")),
            P(("groups", "bricks")),
            P(("groups", "bricks"), None),
        ),
        out_specs=(
            P(("groups", "bricks"), None),
            P(("groups", "bricks"), None),
            P("groups", None, None),
            P("groups", None),
            P("groups", None),
        ),
        check_vma=False,
    )
```
